32 devices in a mesh: expert: 8 (over z, y), tensor: 4 (over x, core).
Axes of the slice: x: 2, y: 2, z: 4, core: 2. Of those that a mesh axis runs over, the one named last changes fastest.
Arguments:
- inputs: bfloat16 [4096, 768], P(('expert', 'tensor')), may hold values from -6 to 6
- projection: bfloat16 [3, 768, 768], P(None, None, 'tensor'), may hold values from -0.21875 to 0.21875
- output_weight: bfloat16 [768, 768], P('tensor'), may hold values from -1.25 to 1.25
- first_gain: float32 [768], replicated, may hold values from 0.1 to 1.9
- second_gain: float32 [768], replicated, may hold values from 0.1 to 1.9
- bias_table: float32 [12, 32], P('tensor'), may hold values from -4 to 4
- bucket_map: int32 [512], replicated, may hold values from 0 to 31, as said below
- router_weight: bfloat16 [768, 8], replicated, may hold values from -0.15625 to 0.15625
- routing: int32 [4096, 2], P(('expert', 'tensor')), may hold values from 0 to 7, all different within a row; in each aligned block of 128 rows (0 to 127, 128 to 255, ...) at most 48 rows name the same one
- expert_up: bfloat16 [8, 768, 3072], P('expert', None, 'tensor'), may hold values from -0.21875 to 0.21875
- expert_down: bfloat16 [8, 3072, 768], P('expert', 'tensor'), may hold values from -0.109375 to 0.109375
- cotangent: bfloat16 [4096, 768], P(('expert', 'tensor')), may hold values from -6 to 6
Outputs:
- result: bfloat16 [4096, 768], P(('expert', 'tensor'))
- grad_inputs: float32 [4096, 768], P(('expert', 'tensor'))
- grad_projection: float32 [3, 768, 768], P(None, None, 'tensor')
- grad_output: float32 [768, 768], P('tensor')
- grad_first: float32 [768], replicated
- grad_second: float32 [768], replicated
- grad_table: float32 [12, 32], P('tensor')
- grad_router: float32 [768, 8], replicated
- grad_up: float32 [8, 768, 3072], P('expert', None, 'tensor')
- grad_down: float32 [8, 3072, 768], P('expert', 'tensor')
The draws below stay inside these ranges and needn't reach their ends.
Inputs may be any that keep to these rules, and one draw needn't show every extreme that they name: `routing`: each row names 2 different experts. In the rows of one device (aligned blocks of 128 rows) no expert is named by more than 48 rows, and in some blocks one expert is named by exactly 48 rows. `bucket_map`: nondecreasing in the distance, 0 at distance 0; every one of the 32 buckets is used.
All inputs are finite; a program needn't handle non-finite values.
Results may differ from the reference program's by a relative error of at most 0.019.
Values may be sent and summed in bfloat16 or wider, within the bound.
A program may use at most 128 MiB of HBM per device.

```python
import math
import jax
import jax.numpy as jnp
import numpy as np
from jax import lax

D = 768
HEADS = 12
HD = 64
FF = 3072
NB = 32
TOP = 2
SEQ_LEN = 512
EXPERTS = 8
TOKENS = 4096
ROWS_DEV = 128
CAP = 48


def draw_bucket_map(key, part):
    key = jax.random.fold_in(key, 11)
    cuts = jax.random.permutation(key, SEQ_LEN - 1)[:NB - 1].astype(jnp.int32) + 1
    distance = jnp.arange(SEQ_LEN, dtype=jnp.int32)
    return jnp.sum((distance[:, None] >= cuts[None, :]).astype(jnp.int32), axis=1).astype(jnp.int32)


def level_of(rng, dims, pieces, smallest, high):
    gain, own = 1.0, jax.random.fold_in(rng, 6)
    for position, blocks in pieces:
        draws = jnp.exp(jax.random.uniform(jax.random.fold_in(own, position), (blocks,), jnp.float32, smallest / len(pieces), high / len(pieces)))
        gain = gain * jnp.repeat(draws, dims[position] // blocks).reshape([-1 if axis == position else 1 for axis in range(len(dims))])
    return gain


def shared_out(rng, own, number, rows, number_of, top, reach, lean):
    order = jax.random.permutation(rng, number_of)
    packed, common = portions_of(number_of, rows * top, reach, lean, True), portions_of(number_of, rows * top, reach, lean, False)
    places = jnp.arange(number_of)

    def named(sizes, turn):
        used = int((sizes > 0).sum())
        fixed = max(1, used // 4)
        passed = fixed + (places - fixed + turn * (used - fixed)) % max(1, number_of - fixed)
        return jnp.zeros((number_of,), jnp.int32).at[order[jnp.where(places < fixed, places, passed)]].set(jnp.asarray(sizes, jnp.int32))

    sizes = jnp.where(number % 4 == 0, named(packed, number // 4), named(common, number - number // 4 - 1))
    mixed = jax.random.permutation(jax.random.fold_in(own, 3), number_of)
    source_of, taker = mixed[0:number_of // 2 * 2:2], mixed[1:number_of // 2 * 2:2]
    room = jnp.minimum(sizes[source_of] - 1, reach - sizes[taker]) // 2
    room = jnp.where((source_of == order[0]) | (taker == order[0]) | (sizes[taker] == 0), 0, jnp.maximum(room, 0))
    passed = jax.random.randint(jax.random.fold_in(own, 4), (number_of // 2,), 0, 1 << 20) % (room + 1)
    sizes = sizes.at[source_of].add(-passed).at[taker].add(passed)
    items = jnp.searchsorted(jnp.cumsum(sizes), jnp.arange(rows * top), side="right").astype(jnp.int32)
    grid = items.reshape(top, rows).T
    grid = grid[jax.random.permutation(jax.random.fold_in(own, 1), rows)]
    turn = jax.random.randint(jax.random.fold_in(own, 2), (rows, 1), 0, top)
    return jnp.take_along_axis(grid, (jnp.arange(top)[None, :] + turn) % top, axis=1)


def portions_of(count, total, most, skew, full):
    weights = [(1 << 20) // math.isqrt(rank ** skew) + 1 for rank in range(1, count + 1)]
    largest = most if full else min(most, max(-(-total // count), total * weights[0] // sum(weights)))
    least = 1 if total - largest >= count - 1 else 0
    counts, rest = [largest] + [least] * (count - 1), total - largest - least * (count - 1)
    while rest > 0:
        movable = [i for i in range(1, count) if counts[i] < largest] or [i for i in range(1, count) if counts[i] < most]
        pool, left = sum([weights[i] for i in movable]), rest
        for i in movable:
            extra = min(most - counts[i], max(1, left * weights[i] // pool), rest)
            counts[i] = counts[i] + extra
            rest = rest - extra
    return np.array(counts)


def bell_draw(rng, dims, width, most, shards=(), kind=jnp.bfloat16):
    gain = level_of(rng, dims, shards, -0.22, 0.18) if shards else 1.0
    values = jax.random.normal(rng, dims, jnp.float32) * width * gain
    return jnp.minimum(jnp.maximum(values, -most), most).astype(kind)


def setup_inputs(seed: int = 0) -> dict:
    seeds = jax.random.split(jax.random.key(seed), 13)
    inputs = bell_draw(seeds[0], (TOKENS, D), 1.0, 6.0, ((0, 32),))
    projection = bell_draw(seeds[1], (3, D, HEADS * HD), D ** -0.5, 0.21875, ((2, 4),))
    output_weight = bell_draw(seeds[2], (HEADS * HD, D), (D // 32) ** -0.5, 1.25, ((0, 4),))
    first_gain = jnp.clip(1.0 + 0.18 * jax.random.normal(seeds[3], (D,), jnp.float32), 0.1, 1.9)
    second_gain = jnp.clip(1.0 + 0.18 * jax.random.normal(seeds[4], (D,), jnp.float32), 0.1, 1.9)
    bias_table = bell_draw(seeds[5], (HEADS, NB), 1.0, 4.0, ((0, 4),), jnp.float32)
    bucket_map = draw_bucket_map(jax.random.fold_in(seeds[12], 71), 0)
    router_weight = bell_draw(seeds[7], (D, EXPERTS), (2 * D) ** -0.5, 0.15625)
    routing_keys = jax.random.split(jax.random.fold_in(seeds[8], 1), TOKENS // ROWS_DEV)
    routing_turns = jax.random.permutation(jax.random.fold_in(seeds[8], 3), TOKENS // ROWS_DEV)
    routing = jax.vmap(lambda own, number: shared_out(jax.random.fold_in(seeds[8], 2), own, number, ROWS_DEV, EXPERTS, TOP, CAP, 2))(routing_keys, routing_turns).reshape((TOKENS, TOP))
    expert_up = bell_draw(seeds[9], (EXPERTS, D, FF), D ** -0.5, 0.21875, ((0, 8), (2, 4)))
    expert_down = bell_draw(seeds[10], (EXPERTS, FF, D), FF ** -0.5, 0.109375, ((0, 8), (1, 4)))
    cotangent = bell_draw(seeds[11], (TOKENS, D), 1.0, 6.0, ((0, 32),))
    return dict(inputs=inputs, projection=projection, output_weight=output_weight, first_gain=first_gain, second_gain=second_gain, bias_table=bias_table, bucket_map=bucket_map, router_weight=router_weight, routing=routing, expert_up=expert_up, expert_down=expert_down, cotangent=cotangent)


@jax.custom_vjp
def low(v):
    return lax.optimization_barrier(v.astype(jnp.bfloat16)).astype(jnp.float32)

@jax.custom_vjp
def low_back(v):
    return v

def low_keep(v):
    return (low(v), None)

def low_pass(kept, grad):
    return (grad,)

def back_keep(v):
    return (v, None)

def back_low(kept, grad):
    return (low(grad),)
low.defvjp(low_keep, low_pass)
low_back.defvjp(back_keep, back_low)
epsilon = 1e-06
negative = -1e+30
highest = lax.Precision.HIGHEST

def normalize(values, scale_gain):
    return values * lax.rsqrt(lax.optimization_barrier(jnp.mean(values * values, axis=-1, keepdims=True)) + epsilon) * scale_gain

def slot_layout(routing):
    blocks = TOKENS // ROWS_DEV
    flat_routes = routing.reshape(blocks, ROWS_DEV * TOP)
    labels = jnp.arange(EXPERTS, dtype=jnp.int32)
    onehot = (flat_routes[:, :, None] == labels[None, None, :]).astype(jnp.int32)
    ranked = lax.optimization_barrier(jnp.sum(onehot * (jnp.cumsum(onehot, axis=1, dtype=jnp.int32) - 1), axis=2)).astype(jnp.int32)
    block_ids = jnp.arange(blocks, dtype=jnp.int32)[:, None]
    slot_ids = ((flat_routes * blocks + block_ids) * CAP + ranked).reshape(TOKENS, TOP).astype(jnp.int32)
    token_ids = jnp.repeat(jnp.arange(TOKENS, dtype=jnp.int32), TOP)
    holder = jnp.zeros((EXPERTS * blocks * CAP,), jnp.int32).at[slot_ids.reshape(-1)].set(token_ids + 1)
    return (slot_ids, holder)

def attend_sequence(queries, key_rows, value_rows, position_bias, causal):
    scaling = HD ** (-0.5)
    scores = jnp.einsum('qhd,khd->hqk', queries, key_rows, precision=highest) * scaling + position_bias
    scores = low_back(scores)
    scores = jnp.where(causal[None], scores, negative)
    weights = jax.nn.softmax(scores, axis=-1)
    context = jnp.einsum('hqk,khd->qhd', low(weights), value_rows, precision=highest)
    return low_back(low(context))

def forward(inputs, projection, output_weight, first_gain, second_gain, bias_table, router_weight, expert_up, expert_down, bucket_map, routing, slot_ids, holder):
    first_normed = low(normalize(inputs, first_gain))
    projected = jnp.einsum('td,cdf->ctf', first_normed, projection, precision=highest)
    projected = low_back(low(projected))
    sequences = TOKENS // SEQ_LEN
    split_heads = projected.reshape(3, sequences, SEQ_LEN, HEADS, HD)
    positions = jnp.arange(SEQ_LEN, dtype=jnp.int32)
    distance = positions[:, None] - positions[None, :]
    causal = distance >= 0
    per_distance = bias_table[:, bucket_map]
    position_bias = per_distance[:, jnp.maximum(distance, 0)]

    def one_sequence(members):
        return attend_sequence(members[0], members[1], members[2], position_bias, causal)
    context = lax.map(jax.checkpoint(one_sequence), (split_heads[0], split_heads[1], split_heads[2]))
    context = context.reshape(TOKENS, HEADS * HD)
    attended = low_back(jnp.dot(context, output_weight, precision=highest))
    middle = inputs + attended
    second_normed = low(normalize(middle, second_gain))
    logits = jnp.dot(second_normed, router_weight, precision=highest)
    gate_values = jax.nn.softmax(jnp.take_along_axis(logits, routing, axis=1), axis=-1)
    filled = holder > 0
    dispatched = jnp.where(filled[:, None], second_normed[jnp.maximum(holder - 1, 0)], 0.0)
    dispatched = low_back(dispatched).reshape(EXPERTS, -1, D)

    def one_expert(members):
        expert_rows, up_matrix, down_matrix = members
        pre_act = low_back(jnp.dot(expert_rows, up_matrix, precision=highest))
        activated = low(jax.nn.gelu(pre_act))
        return low_back(low(jnp.dot(activated, down_matrix, precision=highest)))
    returned = lax.map(jax.checkpoint(one_expert), (dispatched, expert_up, expert_down)).reshape(-1, D)
    picked = returned[slot_ids]
    return middle + lax.optimization_barrier(jnp.sum(gate_values[:, :, None] * picked, axis=1))

def reference(inputs, projection, output_weight, first_gain, second_gain, bias_table, bucket_map, router_weight, routing, expert_up, expert_down, cotangent):
    slot_ids, holder = slot_layout(routing)

    def run(inputs_value, projection_value, output_value, first_value, second_value, table_value, router_value, up_value, down_value):
        return forward(inputs_value, projection_value, output_value, first_value, second_value, table_value, router_value, up_value, down_value, bucket_map, routing, slot_ids, holder)
    result, pullback = jax.vjp(run, inputs.astype(jnp.float32), projection.astype(jnp.float32), output_weight.astype(jnp.float32), first_gain.astype(jnp.float32), second_gain.astype(jnp.float32), bias_table.astype(jnp.float32), router_weight.astype(jnp.float32), expert_up.astype(jnp.float32), expert_down.astype(jnp.float32))
    gradients = pullback(cotangent.astype(jnp.float32))
    return (result.astype(jnp.bfloat16), gradients[0], gradients[1], gradients[2], gradients[3], gradients[4], gradients[5], gradients[6], gradients[7], gradients[8])
```

```python
from functools import partial

import jax
import jax.numpy as jnp
from jax import lax
from jax.experimental import pallas as pl
from jax.experimental.pallas import tpu as pltpu
from jax.sharding import PartitionSpec as P

epsilon = 1e-06
negative = -1e30
highest = lax.Precision.HIGHEST
f32 = jnp.float32
bf16 = jnp.bfloat16
MESH = pl.DeviceIdType.MESH
limit = 50 * 1024 * 1024


def dot(left, right):
    return jnp.dot(left, right, preferred_element_type=f32)


def dot_nt(left, right):
    return lax.dot_general(left, right, (((1,), (1,)), ((), ())), preferred_element_type=f32)


def dot_tn(left, right):
    return lax.dot_general(left, right, (((0,), (0,)), ((), ())), preferred_element_type=f32)


def vmem(count):
    return [pl.BlockSpec(memory_space=pltpu.VMEM)] * count


def dma(*shape):
    return pltpu.SemaphoreType.DMA(shape)


def params(number):
    return pltpu.CompilerParams(
        collective_id=number, has_side_effects=True, vmem_limit_bytes=limit
    )


def remote(source, target, send, recv, where):
    return pltpu.make_async_remote_copy(
        src_ref=source,
        dst_ref=target,
        send_sem=send,
        recv_sem=recv,
        device_id=where,
        device_id_type=MESH,
    )


def greet(places):
    barrier = pltpu.get_barrier_semaphore()
    for where in places:
        pl.semaphore_signal(barrier, inc=1, device_id=where, device_id_type=MESH)
    pl.semaphore_wait(barrier, len(places))


def tensor_partners():
    me = lax.axis_index("tensor")
    core = lax.rem(me, 2)
    return me, core, me + 1 - 2 * core, lax.rem(me + 2, 4)


def gather_kernel(x_ref, o_ref, send, recv, local):
    me, core, near, far = tensor_partners()
    corner = lax.rem(near + 2, 4)
    to_near, to_far = {"tensor": near}, {"tensor": far}
    greet([to_near, to_far])
    copy_far = remote(x_ref, o_ref.at[me], send.at[1], recv.at[1], to_far)
    copy_far.start()
    copy_near = remote(x_ref, o_ref.at[me], send.at[0], recv.at[0], to_near)
    copy_near.start()
    own = pltpu.make_async_copy(x_ref, o_ref.at[me], local)
    own.start()
    remote(x_ref, o_ref.at[far], send.at[1], recv.at[1], to_far).wait_recv()
    relay = remote(o_ref.at[far], o_ref.at[far], send.at[2], recv.at[2], to_near)
    relay.start()
    remote(x_ref, o_ref.at[near], send.at[0], recv.at[0], to_near).wait_recv()
    remote(x_ref, o_ref.at[corner], send.at[2], recv.at[2], to_near).wait_recv()
    own.wait()
    copy_far.wait_send()
    copy_near.wait_send()
    relay.wait_send()


def gather_tensor(rows, number):
    height, width = rows.shape
    return pl.pallas_call(
        gather_kernel,
        out_shape=jax.ShapeDtypeStruct((4, height, width), rows.dtype),
        in_specs=vmem(1),
        out_specs=vmem(1)[0],
        scratch_shapes=[dma(3), dma(3), pltpu.SemaphoreType.DMA],
        compiler_params=params(number),
    )(rows).reshape(4 * height, width)


def scatter_kernel(x_ref, o_ref, got, mid, came, send, recv):
    me, core, near, far = tensor_partners()
    side = me // 2
    to_near, to_far = {"tensor": near}, {"tensor": far}
    greet([to_near, to_far])
    swaps = []
    for part in (0, 1):
        at_x = lax.rem(side + 1 + part, 2)
        swap = remote(
            x_ref.at[at_x, 1 - core], got.at[part], send.at[part], recv.at[part], to_near
        )
        swap.start()
        swaps.append(swap)
    swaps[0].wait_recv()
    mid[...] = (x_ref[1 - side, core].astype(f32) + got[0].astype(f32)).astype(mid.dtype)
    cross = remote(mid, came, send.at[2], recv.at[2], to_far)
    cross.start()
    swaps[1].wait_recv()
    total = x_ref[side, core].astype(f32) + got[1].astype(f32)
    cross.wait_recv()
    o_ref[...] = total + came[...].astype(f32)
    swaps[0].wait_send()
    swaps[1].wait_send()
    cross.wait_send()


def scatter_tensor(rows, number):
    height, width = rows.shape[0] // 4, rows.shape[1]
    return pl.pallas_call(
        scatter_kernel,
        out_shape=jax.ShapeDtypeStruct((height, width), f32),
        in_specs=vmem(1),
        out_specs=vmem(1)[0],
        scratch_shapes=[
            pltpu.VMEM((2, height, width), rows.dtype),
            pltpu.VMEM((height, width), rows.dtype),
            pltpu.VMEM((height, width), rows.dtype),
            dma(3),
            dma(3),
        ],
        compiler_params=params(number),
    )(rows.reshape(2, 2, height, width))


def dispatch_kernel(groups, x_ref, o_ref, es, er, bs, br, ns, nr, cs, cr, local):
    me, core, near, far = tensor_partners()
    corner = lax.rem(near + 2, 4)
    mine = lax.axis_index("expert")
    to_near, to_far = {"tensor": near}, {"tensor": far}
    greet([{"expert": lax.rem(mine + k, groups)} for k in range(1, groups)] + [to_near, to_far])
    own = pltpu.make_async_copy(x_ref.at[:, mine], o_ref.at[:, me, mine], local)
    own.start()
    sends = []
    for k in range(1, groups):
        there = lax.rem(mine + k, groups)
        copy = remote(
            x_ref.at[:, there], o_ref.at[:, me, mine], es.at[k], er.at[k], {"expert": there}
        )
        copy.start()
        sends.append(copy)

    def source(k):
        return lax.rem(mine + groups - k, groups)

    def relay(k):
        place = source(k)
        block = o_ref.at[:, far, place]
        remote(block, block, bs.at[k], br.at[k], to_far).wait_recv()
        copy = remote(block, block, cs.at[k], cr.at[k], to_near)
        copy.start()
        sends.append(copy)

    for k in range(groups):
        place = source(k)
        block = o_ref.at[:, me, place]
        if k == 0:
            own.wait()
        else:
            remote(x_ref.at[:, place], block, es.at[k], er.at[k], {"expert": place}).wait_recv()
        copy = remote(block, block, bs.at[k], br.at[k], to_far)
        copy.start()
        sends.append(copy)
        copy = remote(block, block, ns.at[k], nr.at[k], to_near)
        copy.start()
        sends.append(copy)
        if k > 0:
            relay(k - 1)
    relay(groups - 1)
    for k in range(groups):
        place = source(k)
        block = o_ref.at[:, near, place]
        remote(block, block, ns.at[k], nr.at[k], to_near).wait_recv()
        block = o_ref.at[:, corner, place]
        remote(block, block, cs.at[k], cr.at[k], to_near).wait_recv()
    for copy in sends:
        copy.wait_send()


def dispatch(rows, number):
    kinds, groups, height, width = rows.shape
    return pl.pallas_call(
        partial(dispatch_kernel, groups),
        out_shape=jax.ShapeDtypeStruct((kinds, 4, groups, height, width), rows.dtype),
        in_specs=[pl.BlockSpec(memory_space=pl.ANY)],
        out_specs=pl.BlockSpec(memory_space=pl.ANY),
        scratch_shapes=[dma(groups)] * 8 + [pltpu.SemaphoreType.DMA],
        compiler_params=params(number),
    )(rows)


def collect_kernel(groups, p_ref, g_ref, o_ref, got, mid, came, done, ps, pr, xs, xr, es, er):
    me, core, near, far = tensor_partners()
    side = me // 2
    mine = lax.axis_index("expert")
    to_near, to_far = {"tensor": near}, {"tensor": far}
    greet([{"expert": lax.rem(mine + k, groups)} for k in range(1, groups)] + [to_near, to_far])
    order = list(range(1, groups)) + [0]
    refs = (p_ref, g_ref)
    swaps, sends = {}, []
    for k in order:
        there = lax.rem(mine + k, groups)
        for kind in (0, 1):
            copy = remote(
                refs[kind].at[:, 1 - core, there],
                got.at[kind, :, k],
                ps.at[kind, k],
                pr.at[kind, k],
                to_near,
            )
            copy.start()
            swaps[kind, k] = copy
    crosses = {}

    def finish(k):
        there = lax.rem(mine + k, groups)
        crosses[k].wait_recv()
        for kind in (0, 1):
            total = (
                refs[kind][side, core, there].astype(f32)
                + got[kind, side, k].astype(f32)
                + came[k, kind].astype(f32)
            ).astype(bf16)
            if k:
                done[k, kind] = total
            else:
                o_ref[kind, mine] = total
        if k:
            copy = remote(
                done.at[k], o_ref.at[:, mine], es.at[k], er.at[k], {"expert": there}
            )
            copy.start()
            sends.append(copy)

    for at, k in enumerate(order):
        there = lax.rem(mine + k, groups)
        for kind in (0, 1):
            swaps[kind, k].wait_recv()
            mid[k, kind] = (
                refs[kind][1 - side, core, there].astype(f32)
                + got[kind, 1 - side, k].astype(f32)
            ).astype(bf16)
        copy = remote(mid.at[k], came.at[k], xs.at[k], xr.at[k], to_far)
        copy.start()
        crosses[k] = copy
        if at > 1:
            finish(order[at - 2])
    finish(order[-2])
    finish(order[-1])
    for k in range(1, groups):
        place = lax.rem(mine + groups - k, groups)
        remote(done.at[k], o_ref.at[:, place], es.at[k], er.at[k], {"expert": place}).wait_recv()
    for copy in list(swaps.values()) + list(crosses.values()) + sends:
        copy.wait_send()


def collect(first, second, groups, number):
    height, width = first.shape[0] // (4 * groups), first.shape[1]
    view = (2, 2, groups, height, width)
    return pl.pallas_call(
        partial(collect_kernel, groups),
        out_shape=jax.ShapeDtypeStruct((2, groups, height, width), bf16),
        in_specs=vmem(2),
        out_specs=vmem(1)[0],
        scratch_shapes=[
            pltpu.VMEM((2, 2, groups, height, width), bf16),
            pltpu.VMEM((groups, 2, height, width), bf16),
            pltpu.VMEM((groups, 2, height, width), bf16),
            pltpu.VMEM((groups, 2, height, width), bf16),
            dma(2, groups),
            dma(2, groups),
            dma(groups),
            dma(groups),
            dma(groups),
            dma(groups),
        ],
        compiler_params=params(number),
    )(first.reshape(view), second.reshape(view))


def attention_scores(query, key, bias_row, scaling):
    length = query.shape[0]
    bias = pltpu.roll(
        jnp.broadcast_to(bias_row, (length, length)), 0, 1, stride=1, stride_axis=0
    )
    row_at = lax.broadcasted_iota(jnp.int32, (length, length), 0)
    column_at = lax.broadcasted_iota(jnp.int32, (length, length), 1)
    return jnp.where(column_at <= row_at, dot_nt(query, key) * scaling + bias, negative)


def unit_rows(rows):
    return rows * lax.rsqrt(jnp.mean(rows * rows, axis=-1, keepdims=True) + epsilon)


def forward_kernel(
    heads, size, x_ref, gain_ref, proj_ref, bias_ref, out_w_ref, qkv_ref, context_ref, log_ref, o_ref
):
    normed = (unit_rows(x_ref[...].astype(f32)) * gain_ref[...]).astype(bf16)
    for part in range(3):
        qkv_ref[part] = dot(normed, proj_ref[part]).astype(bf16)
    for head in range(heads):
        columns = slice(head * size, (head + 1) * size)
        scores = attention_scores(
            qkv_ref[0, :, columns],
            qkv_ref[1, :, columns],
            bias_ref[head : head + 1, :],
            size ** (-0.5),
        )
        peak = jnp.max(scores, axis=-1, keepdims=True)
        shifted = jnp.exp(scores - peak)
        total = jnp.sum(shifted, axis=-1, keepdims=True)
        weights = (shifted / total).astype(bf16)
        log_ref[head] = peak + jnp.log(total)
        context_ref[:, columns] = dot(weights, qkv_ref[2, :, columns]).astype(bf16)
    o_ref[...] = dot(context_ref[...], out_w_ref[...]).astype(bf16)


def backward_kernel(
    heads,
    size,
    x_ref,
    gain_ref,
    proj_ref,
    bias_ref,
    out_w_ref,
    qkv_ref,
    context_ref,
    log_ref,
    up_ref,
    grad_proj_ref,
    grad_out_ref,
    far_ref,
    wide_ref,
    first_ref,
    context_grad,
    parts,
):
    length = x_ref.shape[0]
    scaling = size ** (-0.5)
    grad_out_ref[...] = dot_tn(context_ref[...], up_ref[...])
    context_grad[...] = dot_nt(up_ref[...], out_w_ref[...]).astype(bf16)
    row_at = lax.broadcasted_iota(jnp.int32, (length, length), 0)
    column_at = lax.broadcasted_iota(jnp.int32, (length, length), 1)
    flip = (row_at + column_at == length - 1).astype(bf16)
    for head in range(heads):
        columns = slice(head * size, (head + 1) * size)
        query = qkv_ref[0, :, columns]
        key = qkv_ref[1, :, columns]
        value = qkv_ref[2, :, columns]
        pulled = context_grad[:, columns]
        scores = attention_scores(query, key, bias_ref[head : head + 1, :], scaling)
        full = jnp.exp(scores - log_ref[head])
        prob_grad = dot_nt(pulled, value)
        row_dot = jnp.sum(full * prob_grad, axis=-1, keepdims=True)
        score_grad = (full * (prob_grad - row_dot)).astype(bf16)
        parts[2, :, columns] = dot_tn(full.astype(bf16), pulled).astype(bf16)
        parts[0, :, columns] = (scaling * dot(score_grad, key)).astype(bf16)
        parts[1, :, columns] = (scaling * dot_tn(score_grad, query)).astype(bf16)
        turned = pltpu.roll(dot(flip, score_grad), 1, 1, stride=1, stride_axis=0)
        far_ref[head : head + 1, :] = jnp.sum(turned, axis=0, keepdims=True)
    unit = unit_rows(x_ref[...].astype(f32))
    normed = (unit * gain_ref[...]).astype(bf16)
    wide = jnp.zeros((length, x_ref.shape[1]), f32)
    for part in range(3):
        grad_proj_ref[part] = dot_tn(normed, parts[part])
        wide = wide + dot_nt(parts[part], proj_ref[part])
    first_ref[...] = jnp.sum(wide * unit, axis=0, keepdims=True)
    wide_ref[...] = wide.astype(bf16)


def normalize(values, scale_gain):
    return (
        values * lax.rsqrt(jnp.mean(values * values, axis=-1, keepdims=True) + epsilon) * scale_gain
    )


def per_device(
    inputs,
    projection,
    output_weight,
    first_gain,
    second_gain,
    bias_table,
    bucket_map,
    router_weight,
    routing,
    expert_up,
    expert_down,
    cotangent,
):
    local_rows, model = inputs.shape
    experts = router_weight.shape[1]
    route_count = routing.shape[1]
    capacity = max(2, 3 * route_count * local_rows // (2 * experts))
    aligned = capacity % 16 == 0
    length = local_rows * 4
    heads = bias_table.shape[0]
    width = projection.shape[2]
    size = width // heads
    slots = experts * capacity

    expert_ids = jnp.arange(experts, dtype=jnp.int32)
    route_hot = routing[:, :, None] == expert_ids[None, None, :]
    hot = jnp.sum(route_hot, axis=1).astype(bf16)
    before = jnp.tril(jnp.ones((local_rows, local_rows), bf16), -1)
    earlier = dot(before, hot)
    slot_of = jnp.sum(
        jnp.where(
            route_hot,
            earlier[:, None, :] + (expert_ids * capacity).astype(f32)[None, None, :],
            0.0,
        ),
        axis=2,
    ).astype(jnp.int32)
    slot_ids = jnp.arange(slots, dtype=jnp.int32)
    places = [
        (slot_ids[:, None] == slot_of[None, :, number]) for number in range(route_count)
    ]
    to_slots = (places[0] | places[1]).astype(bf16)
    place_hot = [place.astype(bf16) for place in places]

    reverse_map = jnp.roll(bucket_map[::-1], 1)
    reverse_hot = (
        reverse_map[None, :] == jnp.arange(bias_table.shape[1], dtype=jnp.int32)[:, None]
    ).astype(f32)
    bias_rows = jnp.dot(bias_table, reverse_hot, precision=highest)
    gain_row = first_gain[None, :]

    gathered = gather_tensor(inputs, 0)
    qkv, context, logs, attended_part = pl.pallas_call(
        partial(forward_kernel, heads, size),
        out_shape=[
            jax.ShapeDtypeStruct((3, length, width), bf16),
            jax.ShapeDtypeStruct((length, width), bf16),
            jax.ShapeDtypeStruct((heads, length, 1), f32),
            jax.ShapeDtypeStruct((length, model), bf16),
        ],
        in_specs=vmem(5),
        out_specs=vmem(4),
        compiler_params=pltpu.CompilerParams(vmem_limit_bytes=limit),
    )(gathered, gain_row, projection, bias_rows, output_weight)
    attended = scatter_tensor(attended_part, 1)

    middle = inputs.astype(f32) + attended
    second_normed = normalize(middle, second_gain).astype(bf16)
    logits = dot(second_normed, router_weight)
    chosen = jnp.sum(jnp.where(route_hot, logits[:, None, :], 0.0), axis=2)
    gate_values = jax.nn.softmax(chosen, axis=-1)
    upstream = cotangent.astype(f32)
    slot_gate = sum(
        jnp.sum(jnp.where(places[number], gate_values[None, :, number], 0.0), axis=1)
        for number in range(route_count)
    )
    send_rows = dot(to_slots, second_normed).astype(bf16)
    grad_send = (dot(to_slots, cotangent) * slot_gate[:, None]).astype(bf16)
    both = jnp.stack([send_rows, grad_send]).reshape(2, experts, capacity, model)
    if aligned:
        arrived = dispatch(both, 2).reshape(2, 4 * slots, model)
    else:
        arrived = lax.all_to_all(both, "expert", split_axis=1, concat_axis=1, tiled=True)
        arrived = lax.all_gather(arrived, "tensor", axis=1, tiled=False)
        arrived = arrived.reshape(2, 4 * slots, model)
    rows, grads = arrived[0], arrived[1]
    up, down = expert_up[0], expert_down[0]
    pre = dot(rows, up)
    act = jax.nn.gelu(pre).astype(bf16)
    out_part = dot(act, down).astype(bf16)
    act_grad = dot_nt(grads, down)
    _, gelu_pull = jax.vjp(jax.nn.gelu, pre)
    pre_grad = gelu_pull(act_grad)[0].astype(bf16)
    back_part = dot_nt(pre_grad, up).astype(bf16)
    grad_down = dot_tn(act, grads)[None]
    grad_up = dot_tn(rows, pre_grad)[None]
    if aligned:
        returned = collect(out_part, back_part, experts, 3).reshape(2, slots, model)
    else:
        returned = jnp.stack([out_part, back_part])
        returned = lax.psum_scatter(returned, "tensor", scatter_dimension=1, tiled=True)
        returned = returned.reshape(2, experts, capacity, model)
        returned = lax.all_to_all(returned, "expert", split_axis=1, concat_axis=1, tiled=True)
        returned = returned.reshape(2, slots, model)
    picked = [dot_tn(place, returned[0]) for place in place_hot]
    coming = dot_tn(to_slots, returned[1])

    result = (
        middle + gate_values[:, 0:1] * picked[0] + gate_values[:, 1:2] * picked[1]
    ).astype(bf16)
    gate_grad = jnp.stack([jnp.sum(upstream * part, axis=1) for part in picked], axis=1)
    chosen_grad = gate_values * (
        gate_grad - jnp.sum(gate_values * gate_grad, axis=1, keepdims=True)
    )
    logit_grad = jnp.sum(jnp.where(route_hot, chosen_grad[:, :, None], 0.0), axis=1)
    normed_grad = coming + jnp.dot(logit_grad, router_weight.astype(f32).T, precision=highest)
    router_part = jnp.dot(logit_grad.T, second_normed.astype(f32), precision=highest)
    _, norm_pull = jax.vjp(normalize, middle, second_gain)
    middle_back, second_part = norm_pull(normed_grad)
    middle_grad = upstream + middle_back

    rows_grad = gather_tensor(middle_grad.astype(bf16), 4)
    grad_projection, grad_output, far_sum, wide_grad, first_part = pl.pallas_call(
        partial(backward_kernel, heads, size),
        out_shape=[
            jax.ShapeDtypeStruct((3, model, width), f32),
            jax.ShapeDtypeStruct((width, model), f32),
            jax.ShapeDtypeStruct((heads, length), f32),
            jax.ShapeDtypeStruct((length, model), bf16),
            jax.ShapeDtypeStruct((1, model), f32),
        ],
        in_specs=vmem(9),
        out_specs=vmem(5),
        scratch_shapes=[
            pltpu.VMEM((length, width), bf16),
            pltpu.VMEM((3, length, width), bf16),
        ],
        compiler_params=pltpu.CompilerParams(vmem_limit_bytes=limit),
    )(gathered, gain_row, projection, bias_rows, output_weight, qkv, context, logs, rows_grad)
    table_grad = jnp.dot(far_sum, reverse_hot.T, precision=highest)
    own_grad = scatter_tensor(wide_grad, 5)
    _, first_pull = jax.vjp(normalize, inputs.astype(f32), first_gain)
    grad_inputs = middle_grad + first_pull(own_grad)[0]
    tensor_index = lax.axis_index("tensor")
    flat_table = jnp.pad(
        table_grad.reshape(1, -1), ((0, 0), (0, model // 4 - table_grad.size))
    )
    here = jnp.arange(4, dtype=jnp.int32)[:, None] == tensor_index
    table_slots = jnp.where(here, flat_table, 0.0).reshape(1, model)
    small = lax.psum(
        jnp.concatenate([first_part, second_part[None, :], table_slots, router_part], axis=0),
        ("expert", "tensor"),
    )
    own_table = jnp.sum(jnp.where(here, small[2].reshape(4, model // 4), 0.0), axis=0)
    table_grad = own_table[: table_grad.size].reshape(table_grad.shape)
    dense = lax.psum(
        (grad_projection.astype(bf16), grad_output.astype(bf16)),
        "expert",
    )
    return (
        result,
        grad_inputs,
        dense[0].astype(f32),
        dense[1].astype(f32),
        small[0],
        small[1],
        table_grad,
        small[3:].T,
        grad_up,
        grad_down,
    )


def solution(mesh):
    return jax.shard_map(
        per_device,
        mesh=mesh,
        in_specs=(
            P(("expert", "tensor"), None),
            P(None, None, "tensor"),
            P("tensor", None),
            P(),
            P(),
            P("tensor", None),
            P(),
            P(),
            P(("expert", "tensor"), None),
            P("expert", None, "tensor"),
            P("expert", "tensor", None),
            P(("expert", "tensor"), None),
        ),
        out_specs=(
            P(("expert", "tensor"), None),
            P(("expert", "tensor"), None),
            P(None, None, "tensor"),
            P("tensor", None),
            P(),
            P(),
            P("tensor", None),
            P(),
            P("expert", None, "tensor"),
            P("expert", "tensor", None),
        ),
        check_vma=False,
    )
```

```python
from functools import partial

import jax
import jax.numpy as jnp
from jax import lax
from jax.experimental import pallas as pl
from jax.experimental.pallas import tpu as pltpu
from jax.sharding import PartitionSpec as P

epsilon = 1e-06
negative = -1e30
highest = lax.Precision.HIGHEST
f32 = jnp.float32
bf16 = jnp.bfloat16
MESH = pl.DeviceIdType.MESH
limit = 50 * 1024 * 1024


def dot(left, right):
    return jnp.dot(left, right, preferred_element_type=f32)


def dot_nt(left, right):
    return lax.dot_general(left, right, (((1,), (1,)), ((), ())), preferred_element_type=f32)


def dot_tn(left, right):
    return lax.dot_general(left, right, (((0,), (0,)), ((), ())), preferred_element_type=f32)


def vmem(count):
    return [pl.BlockSpec(memory_space=pltpu.VMEM)] * count


def dma(*shape):
    return pltpu.SemaphoreType.DMA(shape)


def params(number):
    return pltpu.CompilerParams(
        collective_id=number, has_side_effects=True, vmem_limit_bytes=limit
    )


def remote(source, target, send, recv, where):
    return pltpu.make_async_remote_copy(
        src_ref=source,
        dst_ref=target,
        send_sem=send,
        recv_sem=recv,
        device_id=where,
        device_id_type=MESH,
    )


def greet(places):
    barrier = pltpu.get_barrier_semaphore()
    for where in places:
        pl.semaphore_signal(barrier, inc=1, device_id=where, device_id_type=MESH)
    pl.semaphore_wait(barrier, len(places))


def tensor_partners():
    me = lax.axis_index("tensor")
    core = lax.rem(me, 2)
    return me, core, me + 1 - 2 * core, lax.rem(me + 2, 4)


def gather_kernel(x_ref, o_ref, send, recv, local):
    me, core, near, far = tensor_partners()
    corner = lax.rem(near + 2, 4)
    to_near, to_far = {"tensor": near}, {"tensor": far}
    greet([to_near, to_far])
    copy_far = remote(x_ref, o_ref.at[me], send.at[1], recv.at[1], to_far)
    copy_far.start()
    copy_near = remote(x_ref, o_ref.at[me], send.at[0], recv.at[0], to_near)
    copy_near.start()
    own = pltpu.make_async_copy(x_ref, o_ref.at[me], local)
    own.start()
    remote(x_ref, o_ref.at[far], send.at[1], recv.at[1], to_far).wait_recv()
    relay = remote(o_ref.at[far], o_ref.at[far], send.at[2], recv.at[2], to_near)
    relay.start()
    remote(x_ref, o_ref.at[near], send.at[0], recv.at[0], to_near).wait_recv()
    remote(x_ref, o_ref.at[corner], send.at[2], recv.at[2], to_near).wait_recv()
    own.wait()
    copy_far.wait_send()
    copy_near.wait_send()
    relay.wait_send()


def gather_tensor(rows, number):
    height, width = rows.shape
    return pl.pallas_call(
        gather_kernel,
        out_shape=jax.ShapeDtypeStruct((4, height, width), rows.dtype),
        in_specs=vmem(1),
        out_specs=vmem(1)[0],
        scratch_shapes=[dma(3), dma(3), pltpu.SemaphoreType.DMA],
        compiler_params=params(number),
    )(rows).reshape(4 * height, width)


def scatter_kernel(x_ref, o_ref, got, mid, came, send, recv):
    me, core, near, far = tensor_partners()
    side = me // 2
    to_near, to_far = {"tensor": near}, {"tensor": far}
    greet([to_near, to_far])
    swaps = []
    for part in (0, 1):
        at_x = lax.rem(side + 1 + part, 2)
        swap = remote(
            x_ref.at[at_x, 1 - core], got.at[part], send.at[part], recv.at[part], to_near
        )
        swap.start()
        swaps.append(swap)
    swaps[0].wait_recv()
    mid[...] = (x_ref[1 - side, core].astype(f32) + got[0].astype(f32)).astype(mid.dtype)
    cross = remote(mid, came, send.at[2], recv.at[2], to_far)
    cross.start()
    swaps[1].wait_recv()
    total = x_ref[side, core].astype(f32) + got[1].astype(f32)
    cross.wait_recv()
    o_ref[...] = total + came[...].astype(f32)
    swaps[0].wait_send()
    swaps[1].wait_send()
    cross.wait_send()


def scatter_tensor(rows, number):
    height, width = rows.shape[0] // 4, rows.shape[1]
    return pl.pallas_call(
        scatter_kernel,
        out_shape=jax.ShapeDtypeStruct((height, width), f32),
        in_specs=vmem(1),
        out_specs=vmem(1)[0],
        scratch_shapes=[
            pltpu.VMEM((2, height, width), rows.dtype),
            pltpu.VMEM((height, width), rows.dtype),
            pltpu.VMEM((height, width), rows.dtype),
            dma(3),
            dma(3),
        ],
        compiler_params=params(number),
    )(rows.reshape(2, 2, height, width))


def dispatch_kernel(groups, x_ref, o_ref, es, er, bs, br, ns, nr, cs, cr, local):
    me, core, near, far = tensor_partners()
    corner = lax.rem(near + 2, 4)
    mine = lax.axis_index("expert")
    to_near, to_far = {"tensor": near}, {"tensor": far}
    greet([{"expert": lax.rem(mine + k, groups)} for k in range(1, groups)] + [to_near, to_far])
    own = pltpu.make_async_copy(x_ref.at[:, mine], o_ref.at[:, me, mine], local)
    own.start()
    sends = []
    for k in range(1, groups):
        there = lax.rem(mine + k, groups)
        copy = remote(
            x_ref.at[:, there], o_ref.at[:, me, mine], es.at[k], er.at[k], {"expert": there}
        )
        copy.start()
        sends.append(copy)

    def source(k):
        return lax.rem(mine + groups - k, groups)

    def relay(k):
        place = source(k)
        block = o_ref.at[:, far, place]
        remote(block, block, bs.at[k], br.at[k], to_far).wait_recv()
        copy = remote(block, block, cs.at[k], cr.at[k], to_near)
        copy.start()
        sends.append(copy)

    for k in range(groups):
        place = source(k)
        block = o_ref.at[:, me, place]
        if k == 0:
            own.wait()
        else:
            remote(x_ref.at[:, place], block, es.at[k], er.at[k], {"expert": place}).wait_recv()
        copy = remote(block, block, bs.at[k], br.at[k], to_far)
        copy.start()
        sends.append(copy)
        copy = remote(block, block, ns.at[k], nr.at[k], to_near)
        copy.start()
        sends.append(copy)
        if k > 0:
            relay(k - 1)
    relay(groups - 1)
    for k in range(groups):
        place = source(k)
        block = o_ref.at[:, near, place]
        remote(block, block, ns.at[k], nr.at[k], to_near).wait_recv()
        block = o_ref.at[:, corner, place]
        remote(block, block, cs.at[k], cr.at[k], to_near).wait_recv()
    for copy in sends:
        copy.wait_send()


def dispatch(rows, number):
    kinds, groups, height, width = rows.shape
    return pl.pallas_call(
        partial(dispatch_kernel, groups),
        out_shape=jax.ShapeDtypeStruct((kinds, 4, groups, height, width), rows.dtype),
        in_specs=[pl.BlockSpec(memory_space=pl.ANY)],
        out_specs=pl.BlockSpec(memory_space=pl.ANY),
        scratch_shapes=[dma(groups)] * 8 + [pltpu.SemaphoreType.DMA],
        compiler_params=params(number),
    )(rows)


def collect_kernel(groups, p_ref, g_ref, o_ref, got, mid, came, done, ps, pr, xs, xr, es, er):
    me, core, near, far = tensor_partners()
    side = me // 2
    mine = lax.axis_index("expert")
    to_near, to_far = {"tensor": near}, {"tensor": far}
    greet([{"expert": lax.rem(mine + k, groups)} for k in range(1, groups)] + [to_near, to_far])
    order = list(range(1, groups)) + [0]
    refs = (p_ref, g_ref)
    swaps, sends = {}, []
    for k in order:
        there = lax.rem(mine + k, groups)
        for kind in (0, 1):
            copy = remote(
                refs[kind].at[:, 1 - core, there],
                got.at[kind, :, k],
                ps.at[kind, k],
                pr.at[kind, k],
                to_near,
            )
            copy.start()
            swaps[kind, k] = copy
    crosses = {}

    def finish(k):
        there = lax.rem(mine + k, groups)
        crosses[k].wait_recv()
        for kind in (0, 1):
            total = (
                refs[kind][side, core, there].astype(f32)
                + got[kind, side, k].astype(f32)
                + came[k, kind].astype(f32)
            ).astype(bf16)
            if k:
                done[k, kind] = total
            else:
                o_ref[kind, mine] = total
        if k:
            copy = remote(
                done.at[k], o_ref.at[:, mine], es.at[k], er.at[k], {"expert": there}
            )
            copy.start()
            sends.append(copy)

    for at, k in enumerate(order):
        there = lax.rem(mine + k, groups)
        for kind in (0, 1):
            swaps[kind, k].wait_recv()
            mid[k, kind] = (
                refs[kind][1 - side, core, there].astype(f32)
                + got[kind, 1 - side, k].astype(f32)
            ).astype(bf16)
        copy = remote(mid.at[k], came.at[k], xs.at[k], xr.at[k], to_far)
        copy.start()
        crosses[k] = copy
        if at > 1:
            finish(order[at - 2])
    finish(order[-2])
    finish(order[-1])
    for k in range(1, groups):
        place = lax.rem(mine + groups - k, groups)
        remote(done.at[k], o_ref.at[:, place], es.at[k], er.at[k], {"expert": place}).wait_recv()
    for copy in list(swaps.values()) + list(crosses.values()) + sends:
        copy.wait_send()


def collect(first, second, groups, number):
    height, width = first.shape[0] // (4 * groups), first.shape[1]
    view = (2, 2, groups, height, width)
    return pl.pallas_call(
        partial(collect_kernel, groups),
        out_shape=jax.ShapeDtypeStruct((2, groups, height, width), bf16),
        in_specs=vmem(2),
        out_specs=vmem(1)[0],
        scratch_shapes=[
            pltpu.VMEM((2, 2, groups, height, width), bf16),
            pltpu.VMEM((groups, 2, height, width), bf16),
            pltpu.VMEM((groups, 2, height, width), bf16),
            pltpu.VMEM((groups, 2, height, width), bf16),
            dma(2, groups),
            dma(2, groups),
            dma(groups),
            dma(groups),
            dma(groups),
            dma(groups),
        ],
        compiler_params=params(number),
    )(first.reshape(view), second.reshape(view))


def finish_kernel(
    groups,
    w_ref,
    d_ref,
    s_ref,
    wide_ref,
    dense_ref,
    small_ref,
    got,
    mid,
    came,
    halves,
    held,
    pieces,
    by_tensor,
    by_expert,
    ws,
    wr,
    ts,
    tr,
    xs,
    xr,
    ys,
    yr,
    zs,
    zr,
    gs,
    gr,
    hs,
    hr,
):
    me, core, near, far = tensor_partners()
    side = me // 2
    mine = lax.axis_index("expert")
    deep = groups // 2
    row, line = lax.rem(mine, 2), mine // 2
    to_near, to_far = {"tensor": near}, {"tensor": far}
    to_row = {"expert": line * 2 + 1 - row}
    chunks = d_ref.shape[0]
    greet(
        [{"expert": lax.rem(mine + k, groups)} for k in range(1, groups)]
        + [{"tensor": lax.rem(me + k, 4)} for k in range(1, 4)]
    )
    sends = []

    def start(*arguments):
        copy = remote(*arguments)
        copy.start()
        sends.append(copy)
        return copy

    for k in range(1, 4):
        start(s_ref, by_tensor.at[me], ts.at[k], tr.at[k], {"tensor": lax.rem(me + k, 4)})
    by_tensor[me] = s_ref[...]
    first = [
        start(d_ref.at[c, 1 - row], halves.at[c], ys.at[c], yr.at[c], to_row)
        for c in range(chunks)
    ]
    swaps = [
        start(
            w_ref.at[lax.rem(side + 1 + part, 2), 1 - core],
            got.at[part],
            ws.at[part],
            wr.at[part],
            to_near,
        )
        for part in (0, 1)
    ]
    for k in range(1, 4):
        there = lax.rem(me + 4 - k, 4)
        remote(s_ref, by_tensor.at[there], ts.at[k], tr.at[k], {"tensor": there}).wait_recv()
    by_expert[mine] = by_tensor[0] + by_tensor[1] + by_tensor[2] + by_tensor[3]
    for k in range(1, groups):
        there = lax.rem(mine + k, groups)
        start(by_expert.at[mine], by_expert.at[mine], xs.at[k], xr.at[k], {"expert": there})
    swaps[0].wait_recv()
    mid[...] = (w_ref[1 - side, core].astype(f32) + got[0].astype(f32)).astype(bf16)
    cross = start(mid, came, ws.at[2], wr.at[2], to_far)

    def along(k):
        return {"expert": lax.rem(line + k, deep) * 2 + row}

    def halve(c):
        first[c].wait_recv()
        held[c] = (d_ref[c, row].astype(f32) + halves[c].astype(f32)).astype(bf16)
        for k in range(1, deep):
            start(
                held.at[c, lax.rem(line + k, deep)],
                pieces.at[c, k],
                zs.at[c, k],
                zr.at[c, k],
                along(k),
            )

    def total(c):
        value = held[c, line].astype(f32)
        for k in range(1, deep):
            remote(
                held.at[c, line], pieces.at[c, k], zs.at[c, k], zr.at[c, k], along(k)
            ).wait_recv()
            value = value + pieces[c, k].astype(f32)
        dense_ref[c, row, line] = value.astype(bf16)
        block = dense_ref.at[c, row, line]
        for k in range(1, deep):
            start(block, block, gs.at[c, k], gr.at[c, k], along(k))

    def spread(c):
        for k in range(1, deep):
            block = dense_ref.at[c, row, lax.rem(line + deep - k, deep)]
            remote(block, block, gs.at[c, k], gr.at[c, k], along(k)).wait_recv()
        start(dense_ref.at[c, row], dense_ref.at[c, row], hs.at[c], hr.at[c], to_row)

    for step in range(chunks + 2):
        for stage, c in ((halve, step), (total, step - 1), (spread, step - 2)):
            if 0 <= c < chunks:
                stage(c)
    swaps[1].wait_recv()
    value = w_ref[side, core].astype(f32) + got[1].astype(f32)
    cross.wait_recv()
    wide_ref[...] = value + came[...].astype(f32)
    for k in range(1, groups):
        place = lax.rem(mine + groups - k, groups)
        block = by_expert.at[place]
        remote(block, block, xs.at[k], xr.at[k], {"expert": place}).wait_recv()
    value = by_expert[0]
    for k in range(1, groups):
        value = value + by_expert[k]
    small_ref[...] = value
    for c in range(chunks):
        block = dense_ref.at[c, 1 - row]
        remote(block, block, hs.at[c], hr.at[c], to_row).wait_recv()
    for copy in sends:
        copy.wait_send()


def finish(wide, dense, small, groups, number):
    height, width = wide.shape[0] // 4, wide.shape[1]
    deep, chunks = groups // 2, 3
    piece = dense.shape[0] // (chunks * groups)
    view = (chunks, 2, deep, piece, width)
    return pl.pallas_call(
        partial(finish_kernel, groups),
        out_shape=[
            jax.ShapeDtypeStruct((height, width), f32),
            jax.ShapeDtypeStruct(view, bf16),
            jax.ShapeDtypeStruct(small.shape, f32),
        ],
        in_specs=vmem(3),
        out_specs=vmem(3),
        scratch_shapes=[
            pltpu.VMEM((2, height, width), bf16),
            pltpu.VMEM((height, width), bf16),
            pltpu.VMEM((height, width), bf16),
            pltpu.VMEM((chunks, deep, piece, width), bf16),
            pltpu.VMEM((chunks, deep, piece, width), bf16),
            pltpu.VMEM((chunks, deep, piece, width), bf16),
            pltpu.VMEM((4,) + small.shape, f32),
            pltpu.VMEM((groups,) + small.shape, f32),
            dma(3),
            dma(3),
            dma(4),
            dma(4),
            dma(groups),
            dma(groups),
            dma(chunks),
            dma(chunks),
            dma(chunks, deep),
            dma(chunks, deep),
            dma(chunks, deep),
            dma(chunks, deep),
            dma(chunks),
            dma(chunks),
        ],
        compiler_params=params(number),
    )(wide.reshape(2, 2, height, width), dense.reshape(view), small)


def attention_scores(query, key, bias_row, scaling):
    length = query.shape[0]
    bias = pltpu.roll(
        jnp.broadcast_to(bias_row, (length, length)), 0, 1, stride=1, stride_axis=0
    )
    row_at = lax.broadcasted_iota(jnp.int32, (length, length), 0)
    column_at = lax.broadcasted_iota(jnp.int32, (length, length), 1)
    return jnp.where(column_at <= row_at, dot_nt(query, key) * scaling + bias, negative)


def unit_rows(rows):
    return rows * lax.rsqrt(jnp.mean(rows * rows, axis=-1, keepdims=True) + epsilon)


def forward_kernel(
    heads, size, x_ref, gain_ref, proj_ref, bias_ref, out_w_ref, qkv_ref, context_ref, log_ref, o_ref
):
    normed = (unit_rows(x_ref[...].astype(f32)) * gain_ref[...]).astype(bf16)
    for part in range(3):
        qkv_ref[part] = dot_nt(normed, proj_ref[part]).astype(bf16)
    for head in range(heads):
        columns = slice(head * size, (head + 1) * size)
        scores = attention_scores(
            qkv_ref[0, :, columns],
            qkv_ref[1, :, columns],
            bias_ref[head : head + 1, :],
            size ** (-0.5),
        )
        peak = jnp.max(scores, axis=-1, keepdims=True)
        shifted = jnp.exp(scores - peak)
        total = jnp.sum(shifted, axis=-1, keepdims=True)
        weights = (shifted / total).astype(bf16)
        log_ref[head] = peak + jnp.log(total)
        context_ref[:, columns] = dot(weights, qkv_ref[2, :, columns]).astype(bf16)
    o_ref[...] = dot(context_ref[...], out_w_ref[...]).astype(bf16)


def backward_kernel(
    heads,
    size,
    x_ref,
    gain_ref,
    proj_ref,
    bias_ref,
    out_w_ref,
    qkv_ref,
    context_ref,
    log_ref,
    up_ref,
    dense_ref,
    far_ref,
    wide_ref,
    first_ref,
    context_grad,
    parts,
):
    length = x_ref.shape[0]
    scaling = size ** (-0.5)
    dense_ref[3] = dot_tn(context_ref[...], up_ref[...]).astype(bf16)
    context_grad[...] = dot_nt(up_ref[...], out_w_ref[...]).astype(bf16)
    row_at = lax.broadcasted_iota(jnp.int32, (length, length), 0)
    column_at = lax.broadcasted_iota(jnp.int32, (length, length), 1)
    flip = (row_at + column_at == length - 1).astype(bf16)
    for head in range(heads):
        columns = slice(head * size, (head + 1) * size)
        query = qkv_ref[0, :, columns]
        key = qkv_ref[1, :, columns]
        value = qkv_ref[2, :, columns]
        pulled = context_grad[:, columns]
        scores = attention_scores(query, key, bias_ref[head : head + 1, :], scaling)
        full = jnp.exp(scores - log_ref[head])
        prob_grad = dot_nt(pulled, value)
        row_dot = jnp.sum(full * prob_grad, axis=-1, keepdims=True)
        score_grad = (full * (prob_grad - row_dot)).astype(bf16)
        parts[2, :, columns] = dot_tn(full.astype(bf16), pulled).astype(bf16)
        parts[0, :, columns] = (scaling * dot(score_grad, key)).astype(bf16)
        parts[1, :, columns] = (scaling * dot_tn(score_grad, query)).astype(bf16)
        turned = pltpu.roll(dot(flip, score_grad), 1, 1, stride=1, stride_axis=0)
        far_ref[head : head + 1, :] = jnp.sum(turned, axis=0, keepdims=True)
    unit = unit_rows(x_ref[...].astype(f32))
    normed = (unit * gain_ref[...]).astype(bf16)
    wide = jnp.zeros((length, x_ref.shape[1]), f32)
    for part in range(3):
        dense_ref[part] = dot_tn(parts[part], normed).astype(bf16)
        wide = wide + dot(parts[part], proj_ref[part])
    first_ref[...] = jnp.sum(wide * unit, axis=0, keepdims=True)
    wide_ref[...] = wide.astype(bf16)


def normalize(values, scale_gain):
    return (
        values * lax.rsqrt(jnp.mean(values * values, axis=-1, keepdims=True) + epsilon) * scale_gain
    )


def per_device(
    inputs,
    projection,
    output_weight,
    first_gain,
    second_gain,
    bias_table,
    bucket_map,
    router_weight,
    routing,
    expert_up,
    expert_down,
    cotangent,
):
    local_rows, model = inputs.shape
    experts = router_weight.shape[1]
    route_count = routing.shape[1]
    capacity = max(2, 3 * route_count * local_rows // (2 * experts))
    aligned = capacity % 16 == 0
    length = local_rows * 4
    heads = bias_table.shape[0]
    width = projection.shape[2]
    size = width // heads
    slots = experts * capacity

    expert_ids = jnp.arange(experts, dtype=jnp.int32)
    route_hot = routing[:, :, None] == expert_ids[None, None, :]
    hot = jnp.sum(route_hot, axis=1).astype(bf16)
    before = jnp.tril(jnp.ones((local_rows, local_rows), bf16), -1)
    earlier = dot(before, hot)
    slot_of = jnp.sum(
        jnp.where(
            route_hot,
            earlier[:, None, :] + (expert_ids * capacity).astype(f32)[None, None, :],
            0.0,
        ),
        axis=2,
    ).astype(jnp.int32)
    slot_ids = jnp.arange(slots, dtype=jnp.int32)
    places = [
        (slot_ids[:, None] == slot_of[None, :, number]) for number in range(route_count)
    ]
    to_slots = (places[0] | places[1]).astype(bf16)
    place_hot = [place.astype(bf16) for place in places]

    reverse_map = jnp.roll(bucket_map[::-1], 1)
    reverse_hot = (
        reverse_map[None, :] == jnp.arange(bias_table.shape[1], dtype=jnp.int32)[:, None]
    ).astype(f32)
    bias_rows = jnp.dot(bias_table, reverse_hot, precision=highest)
    gain_row = first_gain[None, :]
    turned_projection = projection.transpose(0, 2, 1)

    gathered = gather_tensor(inputs, 0)
    qkv, context, logs, attended_part = pl.pallas_call(
        partial(forward_kernel, heads, size),
        out_shape=[
            jax.ShapeDtypeStruct((3, length, width), bf16),
            jax.ShapeDtypeStruct((length, width), bf16),
            jax.ShapeDtypeStruct((heads, length, 1), f32),
            jax.ShapeDtypeStruct((length, model), bf16),
        ],
        in_specs=vmem(5),
        out_specs=vmem(4),
        compiler_params=pltpu.CompilerParams(vmem_limit_bytes=limit),
    )(gathered, gain_row, turned_projection, bias_rows, output_weight)
    attended = scatter_tensor(attended_part, 1)

    middle = inputs.astype(f32) + attended
    second_normed = normalize(middle, second_gain).astype(bf16)
    logits = dot(second_normed, router_weight)
    chosen = jnp.sum(jnp.where(route_hot, logits[:, None, :], 0.0), axis=2)
    gate_values = jax.nn.softmax(chosen, axis=-1)
    upstream = cotangent.astype(f32)
    slot_gate = sum(
        jnp.sum(jnp.where(places[number], gate_values[None, :, number], 0.0), axis=1)
        for number in range(route_count)
    )
    send_rows = dot(to_slots, second_normed).astype(bf16)
    grad_send = (dot(to_slots, cotangent) * slot_gate[:, None]).astype(bf16)
    both = jnp.stack([send_rows, grad_send]).reshape(2, experts, capacity, model)
    if aligned:
        arrived = dispatch(both, 2).reshape(2, 4 * slots, model)
    else:
        arrived = lax.all_to_all(both, "expert", split_axis=1, concat_axis=1, tiled=True)
        arrived = lax.all_gather(arrived, "tensor", axis=1, tiled=False)
        arrived = arrived.reshape(2, 4 * slots, model)
    rows, grads = arrived[0], arrived[1]
    up, down = expert_up[0], expert_down[0]
    pre = dot(rows, up)
    act = jax.nn.gelu(pre).astype(bf16)
    out_part = dot(act, down).astype(bf16)
    act_grad = dot_nt(grads, down)
    _, gelu_pull = jax.vjp(jax.nn.gelu, pre)
    pre_grad = gelu_pull(act_grad)[0].astype(bf16)
    back_part = dot_nt(pre_grad, up).astype(bf16)
    grad_down = dot_tn(act, grads)[None]
    grad_up = dot_tn(rows, pre_grad)[None]
    if aligned:
        returned = collect(out_part, back_part, experts, 3).reshape(2, slots, model)
    else:
        returned = jnp.stack([out_part, back_part])
        returned = lax.psum_scatter(returned, "tensor", scatter_dimension=1, tiled=True)
        returned = returned.reshape(2, experts, capacity, model)
        returned = lax.all_to_all(returned, "expert", split_axis=1, concat_axis=1, tiled=True)
        returned = returned.reshape(2, slots, model)
    picked = [dot_tn(place, returned[0]) for place in place_hot]
    coming = dot_tn(to_slots, returned[1])

    result = (
        middle + gate_values[:, 0:1] * picked[0] + gate_values[:, 1:2] * picked[1]
    ).astype(bf16)
    gate_grad = jnp.stack([jnp.sum(upstream * part, axis=1) for part in picked], axis=1)
    chosen_grad = gate_values * (
        gate_grad - jnp.sum(gate_values * gate_grad, axis=1, keepdims=True)
    )
    logit_grad = jnp.sum(jnp.where(route_hot, chosen_grad[:, :, None], 0.0), axis=1)
    normed_grad = coming + jnp.dot(logit_grad, router_weight.astype(f32).T, precision=highest)
    router_part = jnp.dot(logit_grad.T, second_normed.astype(f32), precision=highest)
    _, norm_pull = jax.vjp(normalize, middle, second_gain)
    middle_back, second_part = norm_pull(normed_grad)
    middle_grad = upstream + middle_back

    rows_grad = gather_tensor(middle_grad.astype(bf16), 4)
    dense_part, far_sum, wide_grad, first_part = pl.pallas_call(
        partial(backward_kernel, heads, size),
        out_shape=[
            jax.ShapeDtypeStruct((4, width, model), bf16),
            jax.ShapeDtypeStruct((heads, length), f32),
            jax.ShapeDtypeStruct((length, model), bf16),
            jax.ShapeDtypeStruct((1, model), f32),
        ],
        in_specs=vmem(9),
        out_specs=vmem(4),
        scratch_shapes=[
            pltpu.VMEM((length, width), bf16),
            pltpu.VMEM((3, length, width), bf16),
        ],
        compiler_params=pltpu.CompilerParams(vmem_limit_bytes=limit),
    )(gathered, gain_row, turned_projection, bias_rows, output_weight, qkv, context, logs, rows_grad)
    table_grad = jnp.dot(far_sum, reverse_hot.T, precision=highest)
    tensor_index = lax.axis_index("tensor")
    flat_table = jnp.pad(
        table_grad.reshape(1, -1), ((0, 0), (0, model // 4 - table_grad.size))
    )
    here = jnp.arange(4, dtype=jnp.int32)[:, None] == tensor_index
    table_slots = jnp.where(here, flat_table, 0.0).reshape(1, model)
    small = jnp.concatenate(
        [
            first_part,
            second_part[None, :],
            table_slots,
            router_part,
            jnp.zeros(((-3 - experts) % 8, model), f32),
        ],
        axis=0,
    )
    dense_rows = dense_part.reshape(4 * width, model)
    if (4 * width) % (48 * experts) == 0:
        own_grad, dense, small = finish(wide_grad, dense_rows, small, experts, 5)
    else:
        own_grad = scatter_tensor(wide_grad, 5)
        small = lax.psum(small, ("expert", "tensor"))
        dense = lax.psum(dense_rows, "expert")
    dense = dense.reshape(4, width, model).astype(f32)
    _, first_pull = jax.vjp(normalize, inputs.astype(f32), first_gain)
    grad_inputs = middle_grad + first_pull(own_grad)[0]
    own_table = jnp.sum(jnp.where(here, small[2].reshape(4, model // 4), 0.0), axis=0)
    table_grad = own_table[: table_grad.size].reshape(table_grad.shape)
    return (
        result,
        grad_inputs,
        dense[:3].transpose(0, 2, 1),
        dense[3],
        small[0],
        small[1],
        table_grad,
        small[3 : 3 + experts].T,
        grad_up,
        grad_down,
    )


def solution(mesh):
    return jax.shard_map(
        per_device,
        mesh=mesh,
        in_specs=(
            P(("expert", "tensor"), None),
            P(None, None, "tensor"),
            P("tensor", None),
            P(),
            P(),
            P("tensor", None),
            P(),
            P(),
            P(("expert", "tensor"), None),
            P("expert", None, "tensor"),
            P("expert", "tensor", None),
            P(("expert", "tensor"), None),
        ),
        out_specs=(
            P(("expert", "tensor"), None),
            P(("expert", "tensor"), None),
            P(None, None, "tensor"),
            P("tensor", None),
            P(),
            P(),
            P("tensor", None),
            P(),
            P("expert", None, "tensor"),
            P("expert", "tensor", None),
        ),
        check_vma=False,
    )
```

```python
from functools import partial

import jax
import jax.numpy as jnp
from jax import lax
from jax.experimental import pallas as pl
from jax.experimental.pallas import tpu as pltpu
from jax.sharding import PartitionSpec as P

epsilon = 1e-06
negative = -1e30
highest = lax.Precision.HIGHEST
f32 = jnp.float32
bf16 = jnp.bfloat16
MESH = pl.DeviceIdType.MESH
limit = 50 * 1024 * 1024


def dot(left, right):
    return jnp.dot(left, right, preferred_element_type=f32)


def dot_nt(left, right):
    return lax.dot_general(left, right, (((1,), (1,)), ((), ())), preferred_element_type=f32)


def dot_tn(left, right):
    return lax.dot_general(left, right, (((0,), (0,)), ((), ())), preferred_element_type=f32)


def vmem(count):
    return [pl.BlockSpec(memory_space=pltpu.VMEM)] * count


def dma(*shape):
    return pltpu.SemaphoreType.DMA(shape)


def params(number):
    return pltpu.CompilerParams(
        collective_id=number, has_side_effects=True, vmem_limit_bytes=limit
    )


def remote(source, target, send, recv, where):
    return pltpu.make_async_remote_copy(
        src_ref=source,
        dst_ref=target,
        send_sem=send,
        recv_sem=recv,
        device_id=where,
        device_id_type=MESH,
    )


def greet(places):
    barrier = pltpu.get_barrier_semaphore()
    for where in places:
        pl.semaphore_signal(barrier, inc=1, device_id=where, device_id_type=MESH)
    pl.semaphore_wait(barrier, len(places))


def tensor_partners():
    me = lax.axis_index("tensor")
    core = lax.rem(me, 2)
    return me, core, me + 1 - 2 * core, lax.rem(me + 2, 4)


def exchange_places(ks, groups):
    mine = lax.axis_index("expert")
    return [{"expert": lax.rem(mine + k, groups)} for k in ks if k] + [
        {"expert": lax.rem(mine + groups - k, groups)} for k in ks if k
    ]


def exchange_start(ks, groups, c_ref, co_ref, es, er, el):
    mine = lax.axis_index("expert")
    copies = []
    for k in ks:
        there = lax.rem(mine + k, groups)
        if k:
            copy = remote(
                c_ref.at[there], co_ref.at[mine], es.at[k], er.at[k], {"expert": there}
            )
        else:
            copy = pltpu.make_async_copy(c_ref.at[mine], co_ref.at[mine], el)
        copy.start()
        copies.append(copy)
    return copies


def exchange_wait(ks, groups, copies, c_ref, co_ref, es, er):
    mine = lax.axis_index("expert")
    for k, copy in zip(ks, copies):
        if k:
            place = lax.rem(mine + groups - k, groups)
            remote(
                c_ref.at[place], co_ref.at[place], es.at[k], er.at[k], {"expert": place}
            ).wait_recv()
            copy.wait_send()
        else:
            copy.wait()


def gather_kernel(ks, groups, *refs):
    if ks:
        x_ref, c_ref, o_ref, co_ref, send, recv, local, es, er, el = refs
    else:
        x_ref, o_ref, send, recv, local = refs
    me, core, near, far = tensor_partners()
    corner = lax.rem(near + 2, 4)
    to_near, to_far = {"tensor": near}, {"tensor": far}
    greet([to_near, to_far] + exchange_places(ks, groups))
    copy_far = remote(x_ref, o_ref.at[me], send.at[1], recv.at[1], to_far)
    copy_far.start()
    copy_near = remote(x_ref, o_ref.at[me], send.at[0], recv.at[0], to_near)
    copy_near.start()
    own = pltpu.make_async_copy(x_ref, o_ref.at[me], local)
    own.start()
    if ks:
        copies = exchange_start(ks, groups, c_ref, co_ref, es, er, el)
    remote(x_ref, o_ref.at[far], send.at[1], recv.at[1], to_far).wait_recv()
    relay = remote(o_ref.at[far], o_ref.at[far], send.at[2], recv.at[2], to_near)
    relay.start()
    remote(x_ref, o_ref.at[near], send.at[0], recv.at[0], to_near).wait_recv()
    remote(x_ref, o_ref.at[corner], send.at[2], recv.at[2], to_near).wait_recv()
    own.wait()
    copy_far.wait_send()
    copy_near.wait_send()
    relay.wait_send()
    if ks:
        exchange_wait(ks, groups, copies, c_ref, co_ref, es, er)


def extra_sems(ks, groups):
    return [dma(groups), dma(groups), pltpu.SemaphoreType.DMA] if ks else []


def gather_tensor(rows, number, ks=(), extra=()):
    height, width = rows.shape
    groups = extra[0].shape[0] if ks else 1
    spaces = [pl.BlockSpec(memory_space=pl.ANY)] * len(extra)
    outs = pl.pallas_call(
        partial(gather_kernel, ks, groups),
        out_shape=[jax.ShapeDtypeStruct((4, height, width), rows.dtype)]
        + [jax.ShapeDtypeStruct(one.shape, one.dtype) for one in extra],
        in_specs=vmem(1) + spaces,
        out_specs=vmem(1) + spaces,
        scratch_shapes=[dma(3), dma(3), pltpu.SemaphoreType.DMA] + extra_sems(ks, groups),
        compiler_params=params(number),
    )(rows, *extra)
    return [outs[0].reshape(4 * height, width)] + list(outs[1:])


def scatter_kernel(ks, groups, *refs):
    if ks:
        x_ref, c_ref, o_ref, co_ref, got, mid, came, send, recv, es, er, el = refs
    else:
        x_ref, o_ref, got, mid, came, send, recv = refs
    me, core, near, far = tensor_partners()
    side = me // 2
    to_near, to_far = {"tensor": near}, {"tensor": far}
    greet([to_near, to_far] + exchange_places(ks, groups))
    swaps = []
    for part in (0, 1):
        at_x = lax.rem(side + 1 + part, 2)
        swap = remote(
            x_ref.at[at_x, 1 - core], got.at[part], send.at[part], recv.at[part], to_near
        )
        swap.start()
        swaps.append(swap)
    if ks:
        copies = exchange_start(ks, groups, c_ref, co_ref, es, er, el)
    swaps[0].wait_recv()
    mid[...] = (x_ref[1 - side, core].astype(f32) + got[0].astype(f32)).astype(mid.dtype)
    cross = remote(mid, came, send.at[2], recv.at[2], to_far)
    cross.start()
    swaps[1].wait_recv()
    total = x_ref[side, core].astype(f32) + got[1].astype(f32)
    cross.wait_recv()
    o_ref[...] = total + came[...].astype(f32)
    swaps[0].wait_send()
    swaps[1].wait_send()
    cross.wait_send()
    if ks:
        exchange_wait(ks, groups, copies, c_ref, co_ref, es, er)


def scatter_tensor(rows, number, ks=(), extra=()):
    height, width = rows.shape[0] // 4, rows.shape[1]
    groups = extra[0].shape[0] if ks else 1
    spaces = [pl.BlockSpec(memory_space=pl.ANY)] * len(extra)
    return pl.pallas_call(
        partial(scatter_kernel, ks, groups),
        out_shape=[jax.ShapeDtypeStruct((height, width), f32)]
        + [jax.ShapeDtypeStruct(one.shape, one.dtype) for one in extra],
        in_specs=vmem(1) + spaces,
        out_specs=vmem(1) + spaces,
        scratch_shapes=[
            pltpu.VMEM((2, height, width), rows.dtype),
            pltpu.VMEM((height, width), rows.dtype),
            pltpu.VMEM((height, width), rows.dtype),
            dma(3),
            dma(3),
        ]
        + extra_sems(ks, groups),
        compiler_params=params(number),
    )(rows.reshape(2, 2, height, width), *extra)


def dispatch_kernel(
    groups, split, x_ref, g_ref, c1_ref, c2_ref, o_ref, go_ref, q_ref, es, er, bs, br, ns, nr, cs, cr, ls
):
    me, core, near, far = tensor_partners()
    corner = lax.rem(near + 2, 4)
    mine = lax.axis_index("expert")
    to_near, to_far = {"tensor": near}, {"tensor": far}
    greet([{"expert": lax.rem(mine + k, groups)} for k in range(1, groups)] + [to_near, to_far])
    targets = (o_ref, go_ref, q_ref)
    sends, locals_ = [], {}

    def start(*arguments):
        copy = remote(*arguments)
        copy.start()
        sends.append(copy)

    def source(k):
        return lax.rem(mine + groups - k, groups)

    for kind, ref in ((0, x_ref), (1, g_ref)):
        own = pltpu.make_async_copy(ref.at[mine], targets[kind].at[me, mine], ls.at[kind, 0])
        own.start()
        locals_[kind, 0] = own
        for k in range(1, groups):
            there = lax.rem(mine + k, groups)
            start(
                ref.at[there],
                targets[kind].at[me, mine],
                es.at[kind, k],
                er.at[kind, k],
                {"expert": there},
            )
    for k in range(groups):
        place = source(k)
        held = (c1_ref if k < split else c2_ref).at[place]
        block = q_ref.at[me, place]
        start(held, block, bs.at[2, k], br.at[2, k], to_far)
        start(held, block, ns.at[2, k], nr.at[2, k], to_near)
        own = pltpu.make_async_copy(held, block, ls.at[2, k])
        own.start()
        locals_[2, k] = own

    def relay(kind, k):
        block = targets[kind].at[far, source(k)]
        remote(block, block, bs.at[kind, k], br.at[kind, k], to_far).wait_recv()
        start(block, block, cs.at[kind, k], cr.at[kind, k], to_near)

    for k in range(groups):
        place = source(k)
        for kind, ref in ((0, x_ref), (1, g_ref)):
            block = targets[kind].at[me, place]
            if k == 0:
                locals_[kind, 0].wait()
            else:
                remote(
                    ref.at[place], block, es.at[kind, k], er.at[kind, k], {"expert": place}
                ).wait_recv()
            start(block, block, bs.at[kind, k], br.at[kind, k], to_far)
            start(block, block, ns.at[kind, k], nr.at[kind, k], to_near)
        relay(2, k)
    for k in range(groups):
        relay(0, k)
        relay(1, k)
    for k in range(groups):
        locals_[2, k].wait()
        for kind in range(3):
            block = targets[kind].at[near, source(k)]
            remote(block, block, ns.at[kind, k], nr.at[kind, k], to_near).wait_recv()
            block = targets[kind].at[corner, source(k)]
            remote(block, block, cs.at[kind, k], cr.at[kind, k], to_near).wait_recv()
    for copy in sends:
        copy.wait_send()


def dispatch(rows, gates, early, late, split, number):
    groups, height, width = rows.shape
    space = pl.BlockSpec(memory_space=pl.ANY)
    return pl.pallas_call(
        partial(dispatch_kernel, groups, split),
        out_shape=[
            jax.ShapeDtypeStruct((4,) + rows.shape, rows.dtype),
            jax.ShapeDtypeStruct((4,) + gates.shape, gates.dtype),
            jax.ShapeDtypeStruct((4,) + rows.shape, rows.dtype),
        ],
        in_specs=[space] * 4,
        out_specs=[space] * 3,
        scratch_shapes=[dma(3, groups)] * 9,
        compiler_params=params(number),
    )(rows, gates, early, late)


def collect_kernel(groups, p_ref, g_ref, o_ref, got, mid, came, done, ps, pr, xs, xr, es, er):
    me, core, near, far = tensor_partners()
    side = me // 2
    mine = lax.axis_index("expert")
    to_near, to_far = {"tensor": near}, {"tensor": far}
    greet([{"expert": lax.rem(mine + k, groups)} for k in range(1, groups)] + [to_near, to_far])
    order = list(range(1, groups)) + [0]
    refs = (p_ref, g_ref)
    swaps, sends = {}, []
    for k in order:
        there = lax.rem(mine + k, groups)
        for kind in (0, 1):
            copy = remote(
                refs[kind].at[:, 1 - core, there],
                got.at[kind, :, k],
                ps.at[kind, k],
                pr.at[kind, k],
                to_near,
            )
            copy.start()
            swaps[kind, k] = copy
    crosses = {}

    def finish(k):
        there = lax.rem(mine + k, groups)
        crosses[k].wait_recv()
        for kind in (0, 1):
            total = (
                refs[kind][side, core, there].astype(f32)
                + got[kind, side, k].astype(f32)
                + came[k, kind].astype(f32)
            ).astype(bf16)
            if k:
                done[k, kind] = total
            else:
                o_ref[kind, mine] = total
        if k:
            copy = remote(
                done.at[k], o_ref.at[:, mine], es.at[k], er.at[k], {"expert": there}
            )
            copy.start()
            sends.append(copy)

    for at, k in enumerate(order):
        there = lax.rem(mine + k, groups)
        for kind in (0, 1):
            swaps[kind, k].wait_recv()
            mid[k, kind] = (
                refs[kind][1 - side, core, there].astype(f32)
                + got[kind, 1 - side, k].astype(f32)
            ).astype(bf16)
        copy = remote(mid.at[k], came.at[k], xs.at[k], xr.at[k], to_far)
        copy.start()
        crosses[k] = copy
        if at > 1:
            finish(order[at - 2])
    finish(order[-2])
    finish(order[-1])
    for k in range(1, groups):
        place = lax.rem(mine + groups - k, groups)
        remote(done.at[k], o_ref.at[:, place], es.at[k], er.at[k], {"expert": place}).wait_recv()
    for copy in list(swaps.values()) + list(crosses.values()) + sends:
        copy.wait_send()


def collect(first, second, groups, number):
    height, width = first.shape[0] // (4 * groups), first.shape[1]
    view = (2, 2, groups, height, width)
    return pl.pallas_call(
        partial(collect_kernel, groups),
        out_shape=jax.ShapeDtypeStruct((2, groups, height, width), bf16),
        in_specs=vmem(2),
        out_specs=vmem(1)[0],
        scratch_shapes=[
            pltpu.VMEM((2, 2, groups, height, width), bf16),
            pltpu.VMEM((groups, 2, height, width), bf16),
            pltpu.VMEM((groups, 2, height, width), bf16),
            pltpu.VMEM((groups, 2, height, width), bf16),
            dma(2, groups),
            dma(2, groups),
            dma(groups),
            dma(groups),
            dma(groups),
            dma(groups),
        ],
        compiler_params=params(number),
    )(first.reshape(view), second.reshape(view))


def finish_kernel(
    groups,
    w_ref,
    d_ref,
    s_ref,
    wide_ref,
    dense_ref,
    small_ref,
    got,
    mid,
    came,
    halves,
    held,
    pieces,
    by_tensor,
    by_expert,
    ws,
    wr,
    ts,
    tr,
    xs,
    xr,
    ys,
    yr,
    zs,
    zr,
    gs,
    gr,
    hs,
    hr,
):
    me, core, near, far = tensor_partners()
    side = me // 2
    mine = lax.axis_index("expert")
    deep = groups // 2
    row, line = lax.rem(mine, 2), mine // 2
    to_near, to_far = {"tensor": near}, {"tensor": far}
    to_row = {"expert": line * 2 + 1 - row}
    chunks = d_ref.shape[0]
    greet(
        [{"expert": lax.rem(mine + k, groups)} for k in range(1, groups)]
        + [{"tensor": lax.rem(me + k, 4)} for k in range(1, 4)]
    )
    sends = []

    def start(*arguments):
        copy = remote(*arguments)
        copy.start()
        sends.append(copy)
        return copy

    for k in range(1, 4):
        start(s_ref, by_tensor.at[me], ts.at[k], tr.at[k], {"tensor": lax.rem(me + k, 4)})
    by_tensor[me] = s_ref[...]
    first = [
        start(d_ref.at[c, 1 - row], halves.at[c], ys.at[c], yr.at[c], to_row)
        for c in range(chunks)
    ]
    swaps = [
        start(
            w_ref.at[lax.rem(side + 1 + part, 2), 1 - core],
            got.at[part],
            ws.at[part],
            wr.at[part],
            to_near,
        )
        for part in (0, 1)
    ]
    for k in range(1, 4):
        there = lax.rem(me + 4 - k, 4)
        remote(s_ref, by_tensor.at[there], ts.at[k], tr.at[k], {"tensor": there}).wait_recv()
    by_expert[mine] = by_tensor[0] + by_tensor[1] + by_tensor[2] + by_tensor[3]
    for k in range(1, groups):
        there = lax.rem(mine + k, groups)
        start(by_expert.at[mine], by_expert.at[mine], xs.at[k], xr.at[k], {"expert": there})
    swaps[0].wait_recv()
    mid[...] = (w_ref[1 - side, core].astype(f32) + got[0].astype(f32)).astype(bf16)
    cross = start(mid, came, ws.at[2], wr.at[2], to_far)

    def along(k):
        return {"expert": lax.rem(line + k, deep) * 2 + row}

    def halve(c):
        first[c].wait_recv()
        held[c] = (d_ref[c, row].astype(f32) + halves[c].astype(f32)).astype(bf16)
        for k in range(1, deep):
            start(
                held.at[c, lax.rem(line + k, deep)],
                pieces.at[c, k],
                zs.at[c, k],
                zr.at[c, k],
                along(k),
            )

    def total(c):
        value = held[c, line].astype(f32)
        for k in range(1, deep):
            remote(
                held.at[c, line], pieces.at[c, k], zs.at[c, k], zr.at[c, k], along(k)
            ).wait_recv()
            value = value + pieces[c, k].astype(f32)
        dense_ref[c, row, line] = value.astype(bf16)
        block = dense_ref.at[c, row, line]
        for k in range(1, deep):
            start(block, block, gs.at[c, k], gr.at[c, k], along(k))

    def spread(c):
        for k in range(1, deep):
            block = dense_ref.at[c, row, lax.rem(line + deep - k, deep)]
            remote(block, block, gs.at[c, k], gr.at[c, k], along(k)).wait_recv()
        start(dense_ref.at[c, row], dense_ref.at[c, row], hs.at[c], hr.at[c], to_row)

    for step in range(chunks + 2):
        for stage, c in ((halve, step), (total, step - 1), (spread, step - 2)):
            if 0 <= c < chunks:
                stage(c)
    swaps[1].wait_recv()
    value = w_ref[side, core].astype(f32) + got[1].astype(f32)
    cross.wait_recv()
    wide_ref[...] = value + came[...].astype(f32)
    for k in range(1, groups):
        place = lax.rem(mine + groups - k, groups)
        block = by_expert.at[place]
        remote(block, block, xs.at[k], xr.at[k], {"expert": place}).wait_recv()
    value = by_expert[0]
    for k in range(1, groups):
        value = value + by_expert[k]
    small_ref[...] = value
    for c in range(chunks):
        block = dense_ref.at[c, 1 - row]
        remote(block, block, hs.at[c], hr.at[c], to_row).wait_recv()
    for copy in sends:
        copy.wait_send()


def finish(wide, dense, small, groups, number):
    height, width = wide.shape[0] // 4, wide.shape[1]
    deep, chunks = groups // 2, 3
    piece = dense.shape[0] // (chunks * groups)
    view = (chunks, 2, deep, piece, width)
    return pl.pallas_call(
        partial(finish_kernel, groups),
        out_shape=[
            jax.ShapeDtypeStruct((height, width), f32),
            jax.ShapeDtypeStruct(view, bf16),
            jax.ShapeDtypeStruct(small.shape, f32),
        ],
        in_specs=vmem(3),
        out_specs=vmem(3),
        scratch_shapes=[
            pltpu.VMEM((2, height, width), bf16),
            pltpu.VMEM((height, width), bf16),
            pltpu.VMEM((height, width), bf16),
            pltpu.VMEM((chunks, deep, piece, width), bf16),
            pltpu.VMEM((chunks, deep, piece, width), bf16),
            pltpu.VMEM((chunks, deep, piece, width), bf16),
            pltpu.VMEM((4,) + small.shape, f32),
            pltpu.VMEM((groups,) + small.shape, f32),
            dma(3),
            dma(3),
            dma(4),
            dma(4),
            dma(groups),
            dma(groups),
            dma(chunks),
            dma(chunks),
            dma(chunks, deep),
            dma(chunks, deep),
            dma(chunks, deep),
            dma(chunks, deep),
            dma(chunks),
            dma(chunks),
        ],
        compiler_params=params(number),
    )(wide.reshape(2, 2, height, width), dense.reshape(view), small)


def attention_scores(query, key, bias_row, scaling):
    length = query.shape[0]
    bias = pltpu.roll(
        jnp.broadcast_to(bias_row, (length, length)), 0, 1, stride=1, stride_axis=0
    )
    row_at = lax.broadcasted_iota(jnp.int32, (length, length), 0)
    column_at = lax.broadcasted_iota(jnp.int32, (length, length), 1)
    return jnp.where(column_at <= row_at, dot_nt(query, key) * scaling + bias, negative)


def unit_rows(rows):
    return rows * lax.rsqrt(jnp.mean(rows * rows, axis=-1, keepdims=True) + epsilon)


def forward_kernel(
    heads, size, x_ref, gain_ref, proj_ref, bias_ref, out_w_ref, qkv_ref, context_ref, log_ref, o_ref
):
    normed = (unit_rows(x_ref[...].astype(f32)) * gain_ref[...]).astype(bf16)
    for part in range(3):
        qkv_ref[part] = dot_nt(normed, proj_ref[part]).astype(bf16)
    for head in range(heads):
        columns = slice(head * size, (head + 1) * size)
        scores = attention_scores(
            qkv_ref[0, :, columns],
            qkv_ref[1, :, columns],
            bias_ref[head : head + 1, :],
            size ** (-0.5),
        )
        peak = jnp.max(scores, axis=-1, keepdims=True)
        shifted = jnp.exp(scores - peak)
        total = jnp.sum(shifted, axis=-1, keepdims=True)
        weights = (shifted / total).astype(bf16)
        log_ref[head] = peak + jnp.log(total)
        context_ref[:, columns] = dot(weights, qkv_ref[2, :, columns]).astype(bf16)
    o_ref[...] = dot(context_ref[...], out_w_ref[...]).astype(bf16)


def backward_kernel(
    heads,
    size,
    x_ref,
    gain_ref,
    proj_ref,
    bias_ref,
    out_w_ref,
    qkv_ref,
    context_ref,
    log_ref,
    up_ref,
    dense_ref,
    far_ref,
    wide_ref,
    first_ref,
    context_grad,
    parts,
):
    length = x_ref.shape[0]
    scaling = size ** (-0.5)
    dense_ref[3] = dot_tn(context_ref[...], up_ref[...]).astype(bf16)
    context_grad[...] = dot_nt(up_ref[...], out_w_ref[...]).astype(bf16)
    row_at = lax.broadcasted_iota(jnp.int32, (length, length), 0)
    column_at = lax.broadcasted_iota(jnp.int32, (length, length), 1)
    flip = (row_at + column_at == length - 1).astype(bf16)
    for head in range(heads):
        columns = slice(head * size, (head + 1) * size)
        query = qkv_ref[0, :, columns]
        key = qkv_ref[1, :, columns]
        value = qkv_ref[2, :, columns]
        pulled = context_grad[:, columns]
        scores = attention_scores(query, key, bias_ref[head : head + 1, :], scaling)
        full = jnp.exp(scores - log_ref[head])
        prob_grad = dot_nt(pulled, value)
        row_dot = jnp.sum(full * prob_grad, axis=-1, keepdims=True)
        score_grad = (full * (prob_grad - row_dot)).astype(bf16)
        parts[2, :, columns] = dot_tn(full.astype(bf16), pulled).astype(bf16)
        parts[0, :, columns] = (scaling * dot(score_grad, key)).astype(bf16)
        parts[1, :, columns] = (scaling * dot_tn(score_grad, query)).astype(bf16)
        turned = pltpu.roll(dot(flip, score_grad), 1, 1, stride=1, stride_axis=0)
        far_ref[head : head + 1, :] = jnp.sum(turned, axis=0, keepdims=True)
    unit = unit_rows(x_ref[...].astype(f32))
    normed = (unit * gain_ref[...]).astype(bf16)
    wide = jnp.zeros((length, x_ref.shape[1]), f32)
    for part in range(3):
        dense_ref[part] = dot_tn(parts[part], normed).astype(bf16)
        wide = wide + dot(parts[part], proj_ref[part])
    first_ref[...] = jnp.sum(wide * unit, axis=0, keepdims=True)
    wide_ref[...] = wide.astype(bf16)


def normalize(values, scale_gain):
    return (
        values * lax.rsqrt(jnp.mean(values * values, axis=-1, keepdims=True) + epsilon) * scale_gain
    )


def per_device(
    inputs,
    projection,
    output_weight,
    first_gain,
    second_gain,
    bias_table,
    bucket_map,
    router_weight,
    routing,
    expert_up,
    expert_down,
    cotangent,
):
    local_rows, model = inputs.shape
    experts = router_weight.shape[1]
    route_count = routing.shape[1]
    capacity = max(2, 3 * route_count * local_rows // (2 * experts))
    aligned = capacity % 16 == 0
    length = local_rows * 4
    heads = bias_table.shape[0]
    width = projection.shape[2]
    size = width // heads
    slots = experts * capacity

    expert_ids = jnp.arange(experts, dtype=jnp.int32)
    route_hot = routing[:, :, None] == expert_ids[None, None, :]
    hot = jnp.sum(route_hot, axis=1).astype(bf16)
    before = jnp.tril(jnp.ones((local_rows, local_rows), bf16), -1)
    earlier = dot(before, hot)
    slot_of = jnp.sum(
        jnp.where(
            route_hot,
            earlier[:, None, :] + (expert_ids * capacity).astype(f32)[None, None, :],
            0.0,
        ),
        axis=2,
    ).astype(jnp.int32)
    slot_ids = jnp.arange(slots, dtype=jnp.int32)
    places = [
        (slot_ids[:, None] == slot_of[None, :, number]) for number in range(route_count)
    ]
    to_slots = (places[0] | places[1]).astype(bf16)
    place_hot = [place.astype(bf16) for place in places]

    reverse_map = jnp.roll(bucket_map[::-1], 1)
    reverse_hot = (
        reverse_map[None, :] == jnp.arange(bias_table.shape[1], dtype=jnp.int32)[:, None]
    ).astype(f32)
    bias_rows = jnp.dot(bias_table, reverse_hot, precision=highest)
    gain_row = first_gain[None, :]
    turned_projection = projection.transpose(0, 2, 1)

    spread = dot(to_slots, cotangent)
    if aligned:
        split = experts // 2
        outgoing = spread.astype(bf16).reshape(experts, capacity, model)
        gathered, early = gather_tensor(inputs, 0, tuple(range(split)), (outgoing,))
    else:
        gathered = gather_tensor(inputs, 0)[0]
    qkv, context, logs, attended_part = pl.pallas_call(
        partial(forward_kernel, heads, size),
        out_shape=[
            jax.ShapeDtypeStruct((3, length, width), bf16),
            jax.ShapeDtypeStruct((length, width), bf16),
            jax.ShapeDtypeStruct((heads, length, 1), f32),
            jax.ShapeDtypeStruct((length, model), bf16),
        ],
        in_specs=vmem(5),
        out_specs=vmem(4),
        compiler_params=pltpu.CompilerParams(vmem_limit_bytes=limit),
    )(gathered, gain_row, turned_projection, bias_rows, output_weight)
    if aligned:
        attended, late = scatter_tensor(
            attended_part, 1, tuple(range(split, experts)), (outgoing,)
        )
    else:
        attended = scatter_tensor(attended_part, 1)[0]

    middle = inputs.astype(f32) + attended
    second_normed = normalize(middle, second_gain).astype(bf16)
    logits = dot(second_normed, router_weight)
    chosen = jnp.sum(jnp.where(route_hot, logits[:, None, :], 0.0), axis=2)
    gate_values = jax.nn.softmax(chosen, axis=-1)
    upstream = cotangent.astype(f32)
    slot_gate = sum(
        jnp.sum(jnp.where(places[number], gate_values[None, :, number], 0.0), axis=1)
        for number in range(route_count)
    )
    send_rows = dot(to_slots, second_normed).astype(bf16)
    if aligned:
        gates = jnp.pad(
            slot_gate.reshape(experts, 1, capacity), ((0, 0), (0, 7), (0, 128 - capacity))
        )
        rows, gates, grads = dispatch(
            send_rows.reshape(experts, capacity, model), gates, early, late, split, 2
        )
        rows = rows.reshape(4 * slots, model)
        gates = gates[:, :, 0, :capacity].reshape(4 * slots, 1)
        grads = (gates * grads.reshape(4 * slots, model).astype(f32)).astype(bf16)
    else:
        grad_send = (spread * slot_gate[:, None]).astype(bf16)
        both = jnp.stack([send_rows, grad_send]).reshape(2, experts, capacity, model)
        arrived = lax.all_to_all(both, "expert", split_axis=1, concat_axis=1, tiled=True)
        arrived = lax.all_gather(arrived, "tensor", axis=1, tiled=False)
        arrived = arrived.reshape(2, 4 * slots, model)
        rows, grads = arrived[0], arrived[1]
    up, down = expert_up[0], expert_down[0]
    pre = dot(rows, up)
    act = jax.nn.gelu(pre).astype(bf16)
    out_part = dot(act, down).astype(bf16)
    act_grad = dot_nt(grads, down)
    _, gelu_pull = jax.vjp(jax.nn.gelu, pre)
    pre_grad = gelu_pull(act_grad)[0].astype(bf16)
    back_part = dot_nt(pre_grad, up).astype(bf16)
    grad_down = dot_tn(act, grads)[None]
    grad_up = dot_tn(rows, pre_grad)[None]
    if aligned:
        returned = collect(out_part, back_part, experts, 3).reshape(2, slots, model)
    else:
        returned = jnp.stack([out_part, back_part])
        returned = lax.psum_scatter(returned, "tensor", scatter_dimension=1, tiled=True)
        returned = returned.reshape(2, experts, capacity, model)
        returned = lax.all_to_all(returned, "expert", split_axis=1, concat_axis=1, tiled=True)
        returned = returned.reshape(2, slots, model)
    picked = [dot_tn(place, returned[0]) for place in place_hot]
    coming = dot_tn(to_slots, returned[1])

    result = (
        middle + gate_values[:, 0:1] * picked[0] + gate_values[:, 1:2] * picked[1]
    ).astype(bf16)
    gate_grad = jnp.stack([jnp.sum(upstream * part, axis=1) for part in picked], axis=1)
    chosen_grad = gate_values * (
        gate_grad - jnp.sum(gate_values * gate_grad, axis=1, keepdims=True)
    )
    logit_grad = jnp.sum(jnp.where(route_hot, chosen_grad[:, :, None], 0.0), axis=1)
    normed_grad = coming + jnp.dot(logit_grad, router_weight.astype(f32).T, precision=highest)
    router_part = jnp.dot(logit_grad.T, second_normed.astype(f32), precision=highest)
    _, norm_pull = jax.vjp(normalize, middle, second_gain)
    middle_back, second_part = norm_pull(normed_grad)
    middle_grad = upstream + middle_back

    rows_grad = gather_tensor(middle_grad.astype(bf16), 4)[0]
    dense_part, far_sum, wide_grad, first_part = pl.pallas_call(
        partial(backward_kernel, heads, size),
        out_shape=[
            jax.ShapeDtypeStruct((4, width, model), bf16),
            jax.ShapeDtypeStruct((heads, length), f32),
            jax.ShapeDtypeStruct((length, model), bf16),
            jax.ShapeDtypeStruct((1, model), f32),
        ],
        in_specs=vmem(9),
        out_specs=vmem(4),
        scratch_shapes=[
            pltpu.VMEM((length, width), bf16),
            pltpu.VMEM((3, length, width), bf16),
        ],
        compiler_params=pltpu.CompilerParams(vmem_limit_bytes=limit),
    )(gathered, gain_row, turned_projection, bias_rows, output_weight, qkv, context, logs, rows_grad)
    table_grad = jnp.dot(far_sum, reverse_hot.T, precision=highest)
    tensor_index = lax.axis_index("tensor")
    flat_table = jnp.pad(
        table_grad.reshape(1, -1), ((0, 0), (0, model // 4 - table_grad.size))
    )
    here = jnp.arange(4, dtype=jnp.int32)[:, None] == tensor_index
    table_slots = jnp.where(here, flat_table, 0.0).reshape(1, model)
    small = jnp.concatenate(
        [
            first_part,
            second_part[None, :],
            table_slots,
            router_part,
            jnp.zeros(((-3 - experts) % 8, model), f32),
        ],
        axis=0,
    )
    dense_rows = dense_part.reshape(4 * width, model)
    if (4 * width) % (48 * experts) == 0:
        own_grad, dense, small = finish(wide_grad, dense_rows, small, experts, 5)
    else:
        own_grad = scatter_tensor(wide_grad, 5)[0]
        small = lax.psum(small, ("expert", "tensor"))
        dense = lax.psum(dense_rows, "expert")
    dense = dense.reshape(4, width, model).astype(f32)
    _, first_pull = jax.vjp(normalize, inputs.astype(f32), first_gain)
    grad_inputs = middle_grad + first_pull(own_grad)[0]
    own_table = jnp.sum(jnp.where(here, small[2].reshape(4, model // 4), 0.0), axis=0)
    table_grad = own_table[: table_grad.size].reshape(table_grad.shape)
    return (
        result,
        grad_inputs,
        dense[:3].transpose(0, 2, 1),
        dense[3],
        small[0],
        small[1],
        table_grad,
        small[3 : 3 + experts].T,
        grad_up,
        grad_down,
    )


def solution(mesh):
    return jax.shard_map(
        per_device,
        mesh=mesh,
        in_specs=(
            P(("expert", "tensor"), None),
            P(None, None, "tensor"),
            P("tensor", None),
            P(),
            P(),
            P("tensor", None),
            P(),
            P(),
            P(("expert", "tensor"), None),
            P("expert", None, "tensor"),
            P("expert", "tensor", None),
            P(("expert", "tensor"), None),
        ),
        out_specs=(
            P(("expert", "tensor"), None),
            P(("expert", "tensor"), None),
            P(None, None, "tensor"),
            P("tensor", None),
            P(),
            P(),
            P("tensor", None),
            P(),
            P("expert", None, "tensor"),
            P("expert", "tensor", None),
        ),
        check_vma=False,
    )
```
